32 devices in a mesh: space: 8 (over z, core), filt: 4 (over y, x).
Axes of the slice: x: 2, y: 2, z: 4, core: 2. Of those that a mesh axis runs over, the one named last changes fastest.
Arguments:
- volume: bfloat16 [4, 16, 256, 512], P(None, 'space', 'filt'), may hold values from -6 to 6
- first_kernel: bfloat16 [32, 4, 3, 3, 3], replicated, may hold values from -0.625 to 0.625
- second_kernel: bfloat16 [64, 32, 2, 2, 2], replicated, may hold values from -0.375 to 0.375
- upstream: bfloat16 [64, 8, 32768], P('filt', None, 'space'), may hold values from -0.03125 to 0.03125
Outputs:
- pooled: bfloat16 [64, 8, 32768], P('filt', None, 'space')
- grad_first: float32 [32, 4, 3, 3, 3], P('filt')
- grad_second: float32 [64, 32, 2, 2, 2], P(None, 'filt')
The draws below stay inside these ranges and needn't reach their ends.
All inputs are finite; a program needn't handle non-finite values.
Results may differ from the reference program's by a relative error of at most 0.013.
Values may be sent and summed in bfloat16 or wider, within the bound.
A program may use at most 256 MiB of HBM per device.

```python
import jax
import jax.numpy as jnp
from jax import lax

CH = 4
F1 = 32
F2 = 64
DZ = 2
NY = 256
NX = 512
NZ = 16
N_SPACE = 8


def levels(own_key, extent, split, least, high):
    gain = 1.0
    for dim, blocks in split:
        heights = jax.random.uniform(jax.random.fold_in(jax.random.fold_in(own_key, 6), dim), (blocks,), jnp.float32, least / len(split), high / len(split))
        gain = gain * jnp.repeat(jnp.exp(heights), extent[dim] // blocks).reshape((-1,) + (1,) * (len(extent) - 1 - dim))
    return gain


def noise(stream_key, extent, spread, most, split=(), held_as=jnp.bfloat16):
    result = jax.random.normal(stream_key, extent, jnp.float32) * spread
    if len(split) > 0:
        result = levels(stream_key, extent, split, -0.22, 0.18) * result
    return jnp.clip(result, min=-most, max=most).astype(held_as)


def setup_inputs(seed: int = 0) -> dict:
    keys = jax.random.split(jax.random.key(seed), 5)
    return {
        "volume": noise(keys[0], (CH, NZ, NY, NX), 1.0, 6.0, ((1, 8), (2, 4))),
        "first_kernel": noise(keys[1], (F1, CH, 3, 3, 3), (CH * 27) ** -0.5, 0.625),
        "second_kernel": noise(keys[2], (F2, F1, 2, 2, 2), (F1 * 8) ** -0.5, 0.375),
        "upstream": noise(keys[3], (F2, NZ // 2, (NY // 2) * (NX // 2)), ((1.0 / (DZ * N_SPACE * NY * NX // 8)) ** 0.5), 0.03125, ((0, 4), (2, 8))),
    }


SLOPE = 0.3
DEPTH_BLOCK = 16


def slab_terms(padded, upstream, first_kernel, second_kernel, start):
    block = lax.dynamic_slice_in_dim(padded, start, DEPTH_BLOCK + 2, 1)
    half = DEPTH_BLOCK // 2
    first_out = jnp.zeros((F1, DEPTH_BLOCK * NY * NX), jnp.float32)
    for shift in range(27):
        depth_step, row_step, col_step = shift // 9, (shift // 3) % 3, shift % 3
        window = block[:, depth_step:depth_step + DEPTH_BLOCK, row_step:row_step + NY, col_step:col_step + NX].reshape(CH, -1)
        first_out = first_out + jnp.dot(first_kernel[:, :, depth_step, row_step, col_step], window, preferred_element_type=jnp.float32)
    active = jnp.where(first_out > 0, first_out, SLOPE * first_out).astype(jnp.bfloat16).reshape(F1, DEPTH_BLOCK, NY, NX)
    total = jnp.zeros((F2, half * (NY // 2) * (NX // 2)), jnp.float32)
    up_block = lax.dynamic_slice_in_dim(upstream, start // 2, half, 1).reshape(F2, -1)
    spread_pieces = []
    second_pieces = []
    for shift in range(8):
        depth_step, row_step, col_step = shift // 4, (shift // 2) % 2, shift % 2
        window = active[:, depth_step::2, row_step::2, col_step::2].reshape(F1, -1)
        total = total + jnp.dot(second_kernel[:, :, depth_step, row_step, col_step], window, preferred_element_type=jnp.float32)
        spread_pieces.append(jnp.dot(second_kernel[:, :, depth_step, row_step, col_step].T, up_block, preferred_element_type=jnp.float32))
        second_pieces.append(jnp.dot(up_block, window.T, preferred_element_type=jnp.float32))
    pooled_block = total.astype(jnp.bfloat16).reshape(F2, half, (NY // 2) * (NX // 2))
    back_flow = jnp.stack(spread_pieces).reshape(2, 2, 2, F1, half, NY // 2, NX // 2)
    back_flow = back_flow.transpose(3, 4, 0, 5, 1, 6, 2).reshape(F1, DEPTH_BLOCK, NY, NX)
    second_term = jnp.stack(second_pieces, axis=-1).reshape(F2, F1, 2, 2, 2)
    slopes = jnp.where(active > 0, 1.0, SLOPE).astype(jnp.float32)
    steered = (back_flow * slopes).astype(jnp.bfloat16).reshape(F1, -1)
    first_pieces = []
    for shift in range(27):
        depth_step, row_step, col_step = shift // 9, (shift // 3) % 3, shift % 3
        window = block[:, depth_step:depth_step + DEPTH_BLOCK, row_step:row_step + NY, col_step:col_step + NX].reshape(CH, -1)
        first_pieces.append(jnp.dot(steered, window.T, preferred_element_type=jnp.float32))
    first_term = jnp.stack(first_pieces, axis=-1).reshape(F1, CH, 3, 3, 3)
    return pooled_block, first_term, second_term


def reference(volume, first_kernel, second_kernel, upstream):
    padded = jnp.pad(volume, ((0, 0), (1, 1), (1, 1), (1, 1)))
    grid_up = upstream.reshape(F2, NZ // 2, NY // 2, NX // 2)

    def step(carry, start):
        pooled_block, first_term, second_term = slab_terms(padded, grid_up, first_kernel, second_kernel, start)
        return (carry[0] + first_term, carry[1] + second_term), pooled_block

    starts = (jnp.arange(NZ // DEPTH_BLOCK) * DEPTH_BLOCK).astype(jnp.int32)
    init = (jnp.zeros((F1, CH, 3, 3, 3), jnp.float32), jnp.zeros((F2, F1, 2, 2, 2), jnp.float32))
    grads, blocks = lax.scan(step, init, starts)
    pooled = blocks.transpose(1, 0, 2, 3).reshape(F2, NZ // 2, (NY // 2) * (NX // 2))
    return pooled, grads[0], grads[1]
```

```python
import jax
import jax.numpy as jnp
import numpy as np
from jax import lax
from jax.experimental import pallas as pl
from jax.experimental.pallas import tpu as pltpu
from jax.sharding import PartitionSpec as P

SLOPE = 0.3
GROUP = 4
TAPS = 128


def tap_table(channels):
    table = np.zeros((TAPS, 8, 4, 4, 4, channels), np.float32)
    for cell in range(8):
        a, b, g = cell // 4, (cell // 2) % 2, cell % 2
        for tap in range(channels * 27):
            c, i, j, k = tap // 27, (tap // 9) % 3, (tap // 3) % 3, tap % 3
            table[tap, cell, g + k, b + j, a + i, c] = 1.0
    return table.reshape(TAPS, 8 * 64 * channels)


def dot(left, right, dims=((1,), (0,)), precision=None):
    return lax.dot_general(left, right, (dims, ((), ())), precision=precision, preferred_element_type=jnp.float32)


def section(vol, before, after, above, below, up, taps, table, second, pooled, grads, cells, first_mat, back_mat, g_first, g_second):
    channels, planes, rows, cols = vol.shape
    window = channels * 4
    half = cols // 2
    lanes = half // 128
    filters = taps.shape[0]
    depth = 8 * filters
    source = lax.broadcasted_iota(jnp.int32, (cols, 4 * half), 0)
    target = lax.broadcasted_iota(jnp.int32, (cols, 4 * half), 1)
    pick = (source == 2 * lax.rem(target, half) + lax.div(target, half) - 1).astype(jnp.float32).astype(jnp.bfloat16)

    for dz in range(4):
        for c in range(channels):
            plane = before[c, 0] if dz == 0 else after[c, 0] if dz == 3 else vol[c, dz - 1]
            spread = dot(plane, pick)
            for lane in range(4 * lanes):
                cells[lane, pl.ds(window + dz * channels + c, rows, stride=window), :] = spread[:, lane * 128:(lane + 1) * 128]
    for edge, at in ((above, 0), (below, window * (rows + 1))):
        spread = dot(edge[...], pick)
        for lane in range(4 * lanes):
            cells[lane, at:at + window, :] = spread[:, lane * 128:(lane + 1) * 128]

    size = 16 * channels * 4
    for cell in range(8):
        first_mat[cell * filters:(cell + 1) * filters, :] = dot(taps[...], table[:, cell * size:(cell + 1) * size]).astype(jnp.bfloat16)
    back_mat[...] = second[...].astype(jnp.float32).T.astype(jnp.bfloat16)
    g_first[...] = jnp.zeros_like(g_first)
    g_second[...] = jnp.zeros_like(g_second)
    per_part = up.shape[2] // (GROUP * half)

    def step(index, carry):
        columns = []
        for y in range(GROUP):
            start = pl.multiple_of((index * GROUP + y) * 2 * window, 2 * window)
            tiles = [
                jnp.concatenate(
                    [cells[dx * lanes + lane, pl.ds(start, 4 * window), :].astype(jnp.bfloat16) for lane in range(lanes)], axis=1
                )
                for dx in range(4)
            ]
            columns.append(jnp.concatenate(tiles, axis=0))
        patches = jnp.concatenate(columns, axis=1)
        part = index // per_part
        span = pl.ds(pl.multiple_of((index % per_part) * GROUP * half, GROUP * half), GROUP * half)
        first_out = dot(first_mat[...], patches)
        active = jnp.where(first_out > 0, first_out, SLOPE * first_out).astype(jnp.bfloat16)
        pooled[part, :, span] = dot(second[...], active).astype(jnp.bfloat16)
        gradient = up[part, :, span]
        back_flow = dot(back_mat[...], gradient)
        steered = (back_flow * jnp.where(active.astype(jnp.float32) > 0, 1.0, SLOPE)).astype(jnp.bfloat16)
        g_second[...] += dot(gradient, active, ((1,), (1,)))
        g_first[...] += dot(steered, patches, ((1,), (1,)))
        return carry

    lax.fori_loop(0, rows // 2 // GROUP, step, 0)
    outputs = second.shape[0]
    grads[0:outputs, :] = g_second[...]
    total = jnp.zeros((filters, TAPS), jnp.float32)
    for cell in range(8):
        part = table[:, cell * size:(cell + 1) * size].astype(jnp.float32)
        total += dot(g_first[cell * filters:(cell + 1) * filters, :], part, ((1,), (1,)), lax.Precision.HIGHEST)
    grads[outputs:outputs + filters, :] = jnp.concatenate([total, jnp.zeros((filters, depth - TAPS), jnp.float32)], axis=1)


def halo(cells, axis, dim):
    count = lax.axis_size(axis)
    ends = count - 1
    head = lax.slice_in_dim(cells, 0, 1, axis=dim)
    tail = lax.slice_in_dim(cells, cells.shape[dim] - 1, cells.shape[dim], axis=dim)
    return (
        lax.ppermute(tail, axis, [(i, i + 1) for i in range(ends)]),
        lax.ppermute(head, axis, [(i + 1, i) for i in range(ends)]),
    )


def shards(volume, first_kernel, second_kernel, upstream):
    space, groups = lax.axis_size("space"), lax.axis_size("filt")
    channels, planes, rows, cols = volume.shape
    filters, outputs = first_kernel.shape[0], second_kernel.shape[0]
    group_out, depth_out, band = upstream.shape
    parts = space // groups
    half = cols // 2

    before, after = halo(volume, "space", 1)
    edges = lambda at: jnp.concatenate([a[:, :, at] for a in (before, volume, after)], axis=1).transpose(1, 0, 2)
    ends = groups - 1
    above = lax.ppermute(edges(rows - 1), "filt", [(i, i + 1) for i in range(ends)]).reshape(4 * channels, cols)
    below = lax.ppermute(edges(0), "filt", [(i + 1, i) for i in range(ends)]).reshape(4 * channels, cols)

    sent = upstream.transpose(1, 0, 2)
    sent = lax.all_to_all(sent, "space", 0, 0, tiled=True).reshape(groups, parts, group_out, band)
    sent = lax.all_to_all(sent, "filt", 0, 0, tiled=True)
    up = sent.transpose(1, 0, 2, 3).reshape(parts, outputs, band)

    taps = jnp.pad(first_kernel.reshape(filters, channels * 27), ((0, 0), (0, TAPS - channels * 27)))
    table = jnp.asarray(tap_table(channels), jnp.bfloat16)
    second = second_kernel.transpose(0, 2, 3, 4, 1).reshape(outputs, 8 * filters)
    window = 4 * channels
    vmem = pl.BlockSpec(memory_space=pltpu.VMEM)
    pooled, grads = pl.pallas_call(
        section,
        out_shape=(
            jax.ShapeDtypeStruct((parts, outputs, band), jnp.bfloat16),
            jax.ShapeDtypeStruct((outputs + filters, 8 * filters), jnp.float32),
        ),
        in_specs=[vmem] * 9,
        out_specs=(vmem, vmem),
        scratch_shapes=[
            pltpu.VMEM((4 * half // 128, window * (rows + 2), 128), jnp.float32),
            pltpu.VMEM((8 * filters, 16 * window), jnp.bfloat16),
            pltpu.VMEM((8 * filters, outputs), jnp.bfloat16),
            pltpu.VMEM((8 * filters, 16 * window), jnp.float32),
            pltpu.VMEM((outputs, 8 * filters), jnp.float32),
        ],
        compiler_params=pltpu.CompilerParams(vmem_limit_bytes=48 * 2**20),
        cost_estimate=pl.CostEstimate(flops=6 * 10**9, bytes_accessed=4 * 10**6, transcendentals=0),
        name="section",
    )(volume, before, after, above, below, up, taps, table, second)

    moved = pooled.reshape(parts, groups, group_out, band).transpose(1, 0, 2, 3)
    moved = lax.all_to_all(moved, "filt", 0, 0, tiled=True).reshape(space, group_out, band)
    moved = lax.all_to_all(moved, "space", 0, 0, tiled=True)
    grads = lax.psum(grads, ("space", "filt"))
    offset = lax.axis_index("filt") * (filters // groups)
    own = filters // groups
    grad_first = lax.dynamic_slice(grads, (outputs + offset, 0), (own, channels * 27)).reshape(own, channels, 3, 3, 3)
    grad_second = lax.dynamic_slice_in_dim(grads[:outputs].reshape(outputs, 2, 2, 2, filters), offset, own, 4).transpose(0, 4, 1, 2, 3)
    return (moved.transpose(1, 0, 2), grad_first, grad_second)


def solution(mesh):
    in_specs = (P(None, "space", "filt", None), P(), P(), P("filt", None, "space"))
    out_specs = (
        P("filt", None, "space"),
        P("filt", None, None, None, None),
        P(None, "filt", None, None, None),
    )
    return jax.shard_map(shards, mesh=mesh, in_specs=in_specs, out_specs=out_specs, check_vma=False)
```

```python
import functools

import jax
import jax.numpy as jnp
import numpy as np
from jax import lax
from jax.experimental import pallas as pl
from jax.experimental.pallas import tpu as pltpu
from jax.sharding import PartitionSpec as P

SLOPE = 0.3
GROUP = 4
TAPS = 128
MESH = pl.DeviceIdType.MESH


def tap_table(channels):
    table = np.zeros((TAPS, 8, 4, 4, 4, channels), np.float32)
    for cell in range(8):
        a, b, g = cell // 4, (cell // 2) % 2, cell % 2
        for tap in range(channels * 27):
            c, i, j, k = tap // 27, (tap // 9) % 3, (tap // 3) % 3, tap % 3
            table[tap, cell, g + k, b + j, a + i, c] = 1.0
    return table.reshape(TAPS, 8 * 64 * channels)


def dot(left, right, dims=((1,), (0,)), precision=None):
    return lax.dot_general(left, right, (dims, ((), ())), precision=precision, preferred_element_type=jnp.float32)


def section(vol, before, after, above, below, up, taps, table, second, pooled, grads, cells, first_mat, back_mat, g_first, g_second):
    channels, planes, rows, cols = vol.shape
    window = channels * 4
    half = cols // 2
    lanes = half // 128
    filters = taps.shape[0]
    depth = 8 * filters
    source = lax.broadcasted_iota(jnp.int32, (cols, 4 * half), 0)
    target = lax.broadcasted_iota(jnp.int32, (cols, 4 * half), 1)
    pick = (source == 2 * lax.rem(target, half) + lax.div(target, half) - 1).astype(jnp.float32).astype(jnp.bfloat16)

    for dz in range(4):
        for c in range(channels):
            plane = before[c] if dz == 0 else after[c] if dz == 3 else vol[c, dz - 1]
            spread = dot(plane, pick)
            for lane in range(4 * lanes):
                cells[lane, pl.ds(window + dz * channels + c, rows, stride=window), :] = spread[:, lane * 128:(lane + 1) * 128]
    for edge, at in ((above, 0), (below, window * (rows + 1))):
        spread = dot(edge[...], pick)
        for lane in range(4 * lanes):
            cells[lane, at:at + window, :] = spread[:, lane * 128:(lane + 1) * 128]

    size = 16 * channels * 4
    for cell in range(8):
        first_mat[cell * filters:(cell + 1) * filters, :] = dot(taps[...], table[:, cell * size:(cell + 1) * size]).astype(jnp.bfloat16)
    back_mat[...] = second[...].astype(jnp.float32).T.astype(jnp.bfloat16)
    g_first[...] = jnp.zeros_like(g_first)
    g_second[...] = jnp.zeros_like(g_second)
    groups, _, group_out, band = up.shape
    own = filters // groups
    outputs = second.shape[0]
    per_part = band // (GROUP * half)

    def step(index, carry):
        columns = []
        for y in range(GROUP):
            start = pl.multiple_of((index * GROUP + y) * 2 * window, 2 * window)
            tiles = [
                jnp.concatenate(
                    [cells[dx * lanes + lane, pl.ds(start, 4 * window), :].astype(jnp.bfloat16) for lane in range(lanes)], axis=1
                )
                for dx in range(4)
            ]
            columns.append(jnp.concatenate(tiles, axis=0))
        patches = jnp.concatenate(columns, axis=1)
        part = index // per_part
        span = pl.ds(pl.multiple_of((index % per_part) * GROUP * half, GROUP * half), GROUP * half)
        first_out = dot(first_mat[...], patches)
        active = jnp.where(first_out > 0, first_out, SLOPE * first_out).astype(jnp.bfloat16)
        pooled_tile = dot(second[...], active).astype(jnp.bfloat16)
        for group in range(groups):
            pooled[group, part, :, span] = pooled_tile[group * group_out:(group + 1) * group_out]
        gradient = jnp.concatenate([up[group, part, :, span] for group in range(groups)], axis=0)
        back_flow = dot(back_mat[...], gradient)
        steered = (back_flow * jnp.where(active.astype(jnp.float32) > 0, 1.0, SLOPE)).astype(jnp.bfloat16)
        g_second[...] += dot(active, gradient, ((1,), (1,)))
        g_first[...] += dot(steered, patches, ((1,), (1,)))
        return carry

    lax.fori_loop(0, rows // 2 // GROUP, step, 0)
    grads[...] = jnp.zeros_like(grads)
    total = jnp.zeros((filters, TAPS), jnp.float32)
    for cell in range(8):
        part = table[:, cell * size:(cell + 1) * size].astype(jnp.float32)
        total += dot(g_first[cell * filters:(cell + 1) * filters, :], part, ((1,), (1,)), lax.Precision.HIGHEST)
    for group in range(groups):
        for cell in range(8):
            first = cell * filters + group * own
            grads[group, cell, :, 0:outputs] = g_second[first:first + own, :]
        grads[group, 8, :, :] = total[group * own:(group + 1) * own]


def greet(space, groups, s, f):
    barrier = pltpu.get_barrier_semaphore()
    for d in range(1, space):
        pl.semaphore_signal(barrier, inc=1, device_id=(lax.rem(s + d, space), f), device_id_type=MESH)
    for e in range(1, groups):
        pl.semaphore_signal(barrier, inc=1, device_id=(s, lax.rem(f + e, groups)), device_id_type=MESH)
    pl.semaphore_wait(barrier, space + groups - 2)


def push(source, target, sems, index, device):
    send, recv = sems
    return pltpu.make_async_remote_copy(
        src_ref=source, dst_ref=target, send_sem=send.at[index], recv_sem=recv.at[index], device_id=device, device_id_type=MESH
    )


def when_sent(there, here, copy):
    @pl.when(there)
    def _():
        copy.wait_send()

    @pl.when(here)
    def _():
        copy.wait_recv()


def halo(s, count, ahead, back, filled, emptied):
    @pl.when(s < count - 1)
    def _():
        ahead.start()

    @pl.when(s > 0)
    def _():
        back.start()

    @pl.when(s == 0)
    def _():
        filled[...] = jnp.zeros_like(filled)

    @pl.when(s == count - 1)
    def _():
        emptied[...] = jnp.zeros_like(emptied)


def collect(space, groups, vol, up, before, after, above, below, up_out, mid, tail, head, h_send, h_recv, z_send, z_recv, f_send, f_recv):
    s, f = lax.axis_index("space"), lax.axis_index("filt")
    channels, planes, rows, cols = vol.shape
    parts = space // groups
    greet(space, groups, s, f)
    sems = (h_send, h_recv)
    ahead = push(vol.at[:, planes - 1], before, sems, 0, (jnp.minimum(s + 1, space - 1), f))
    back = push(vol.at[:, 0], after, sems, 1, (jnp.maximum(s - 1, 0), f))
    halo(s, space, ahead, back, before, after)
    moves = []
    for d in range(1, space):
        peer = lax.rem(s + d, space)
        moves.append(push(up.at[peer], mid.at[s], (z_send, z_recv), d, (peer, f)))
        moves[-1].start()
    mid[s] = up[s]
    when_sent(s < space - 1, s > 0, ahead)
    when_sent(s > 0, s < space - 1, back)

    def edge(row):
        lines = [
            (before[c] if dz == 0 else after[c] if dz == 3 else vol[c, dz - 1])[row:row + 1, :].astype(jnp.float32)
            for dz in range(4)
            for c in range(channels)
        ]
        return jnp.concatenate(lines, axis=0).astype(jnp.bfloat16)

    tail[...] = edge(rows - 1)
    head[...] = edge(0)
    down = push(tail, above, sems, 2, (s, jnp.minimum(f + 1, groups - 1)))
    upward = push(head, below, sems, 3, (s, jnp.maximum(f - 1, 0)))
    halo(f, groups, down, upward, above, below)
    for move in moves:
        move.wait()
    turns = []
    for e in range(1, groups):
        peer = lax.rem(f + e, groups)
        turns.append(push(mid.at[pl.ds(peer * parts, parts)], up_out.at[f], (f_send, f_recv), e, (s, peer)))
        turns[-1].start()
    up_out[f] = mid[pl.ds(f * parts, parts)]
    when_sent(f < groups - 1, f > 0, down)
    when_sent(f > 0, f < groups - 1, upward)
    for turn in turns:
        turn.wait()


def deliver(space, groups, pooled, grads, moved, sums, mid, g_mid, g_sum, g_all, f_send, f_recv, z_send, z_recv, gf_send, gf_recv, gz_send, gz_recv):
    s, f = lax.axis_index("space"), lax.axis_index("filt")
    parts = space // groups
    greet(space, groups, s, f)
    turns, g_turns = [], []
    for e in range(1, groups):
        peer = lax.rem(f + e, groups)
        g_turns.append(push(grads.at[peer], g_mid.at[f], (gf_send, gf_recv), e, (s, peer)))
        g_turns[-1].start()
    for e in range(1, groups):
        peer = lax.rem(f + e, groups)
        turns.append(push(pooled.at[peer], mid.at[pl.ds(f * parts, parts)], (f_send, f_recv), e, (s, peer)))
        turns[-1].start()
    g_mid[f] = grads[f]
    mid[pl.ds(f * parts, parts)] = pooled[f]
    for turn in g_turns:
        turn.wait()
    total = g_mid[0]
    for group in range(1, groups):
        total = total + g_mid[group]
    g_sum[...] = total
    g_moves = []
    for d in range(1, space):
        peer = lax.rem(s + d, space)
        g_moves.append(push(g_sum, g_all.at[s], (gz_send, gz_recv), d, (peer, f)))
        g_moves[-1].start()
    g_all[s] = total
    for turn in turns:
        turn.wait()
    moves = []
    for d in range(1, space):
        peer = lax.rem(s + d, space)
        moves.append(push(mid.at[peer], moved.at[s], (z_send, z_recv), d, (peer, f)))
        moves[-1].start()
    moved[s] = mid[s]
    for move in g_moves:
        move.wait()
    total = g_all[0]
    for place in range(1, space):
        total = total + g_all[place]
    sums[...] = total
    for move in moves:
        move.wait()


def shards(volume, first_kernel, second_kernel, upstream):
    space, groups = lax.axis_size("space"), lax.axis_size("filt")
    channels, planes, rows, cols = volume.shape
    filters, outputs = first_kernel.shape[0], second_kernel.shape[0]
    group_out, depth_out, band = upstream.shape
    parts = space // groups
    own = filters // groups
    half = cols // 2
    window = 4 * channels
    vmem = pl.BlockSpec(memory_space=pltpu.VMEM)
    half_type = lambda *shape: jax.ShapeDtypeStruct(shape, jnp.bfloat16)
    dma = lambda *counts: [pltpu.SemaphoreType.DMA((count,)) for count in counts for _ in range(2)]

    before, after, above, below, up = pl.pallas_call(
        functools.partial(collect, space, groups),
        out_shape=(
            half_type(channels, rows, cols),
            half_type(channels, rows, cols),
            half_type(window, cols),
            half_type(window, cols),
            half_type(groups, parts, group_out, band),
        ),
        in_specs=[vmem] * 2,
        out_specs=(vmem,) * 5,
        scratch_shapes=[
            pltpu.VMEM((space, group_out, band), jnp.bfloat16),
            pltpu.VMEM((window, cols), jnp.bfloat16),
            pltpu.VMEM((window, cols), jnp.bfloat16),
            *dma(4, space, groups),
        ],
        compiler_params=pltpu.CompilerParams(collective_id=0, has_side_effects=True, vmem_limit_bytes=32 * 2**20),
        cost_estimate=pl.CostEstimate(flops=10**6, bytes_accessed=10**8, transcendentals=0),
        name="collect",
    )(volume, upstream.transpose(1, 0, 2))

    taps = jnp.pad(first_kernel.reshape(filters, channels * 27), ((0, 0), (0, TAPS - channels * 27)))
    table = jnp.asarray(tap_table(channels), jnp.bfloat16)
    second = second_kernel.transpose(0, 2, 3, 4, 1).reshape(outputs, 8 * filters)
    pooled, grads = pl.pallas_call(
        section,
        out_shape=(
            half_type(groups, parts, group_out, band),
            jax.ShapeDtypeStruct((groups, 9, own, TAPS), jnp.float32),
        ),
        in_specs=[vmem] * 9,
        out_specs=(vmem, vmem),
        scratch_shapes=[
            pltpu.VMEM((4 * half // 128, window * (rows + 2), 128), jnp.float32),
            pltpu.VMEM((8 * filters, 16 * window), jnp.bfloat16),
            pltpu.VMEM((8 * filters, outputs), jnp.bfloat16),
            pltpu.VMEM((8 * filters, 16 * window), jnp.float32),
            pltpu.VMEM((8 * filters, outputs), jnp.float32),
        ],
        compiler_params=pltpu.CompilerParams(vmem_limit_bytes=48 * 2**20),
        cost_estimate=pl.CostEstimate(flops=6 * 10**9, bytes_accessed=4 * 10**6, transcendentals=0),
        name="section",
    )(volume, before, after, above, below, up, taps, table, second)

    moved, sums = pl.pallas_call(
        functools.partial(deliver, space, groups),
        out_shape=(half_type(space, group_out, band), jax.ShapeDtypeStruct((9, own, TAPS), jnp.float32)),
        in_specs=[vmem] * 2,
        out_specs=(vmem, vmem),
        scratch_shapes=[
            pltpu.VMEM((space, group_out, band), jnp.bfloat16),
            pltpu.VMEM((groups, 9, own, TAPS), jnp.float32),
            pltpu.VMEM((9, own, TAPS), jnp.float32),
            pltpu.VMEM((space, 9, own, TAPS), jnp.float32),
            *dma(groups, space, groups, space),
        ],
        compiler_params=pltpu.CompilerParams(collective_id=1, has_side_effects=True, vmem_limit_bytes=32 * 2**20),
        cost_estimate=pl.CostEstimate(flops=10**6, bytes_accessed=10**8, transcendentals=0),
        name="deliver",
    )(pooled, grads)
    grad_first = sums[8, :, 0:channels * 27].reshape(own, channels, 3, 3, 3)
    grad_second = sums[0:8, :, 0:outputs].transpose(2, 1, 0).reshape(outputs, own, 2, 2, 2)
    return (moved.transpose(1, 0, 2), grad_first, grad_second)


def solution(mesh):
    in_specs = (P(None, "space", "filt", None), P(), P(), P("filt", None, "space"))
    out_specs = (
        P("filt", None, "space"),
        P("filt", None, None, None, None),
        P(None, "filt", None, None, None),
    )
    return jax.shard_map(shards, mesh=mesh, in_specs=in_specs, out_specs=out_specs, check_vma=False)
```

```python
import functools

import jax
import jax.numpy as jnp
import numpy as np
from jax import lax
from jax.experimental import pallas as pl
from jax.experimental.pallas import tpu as pltpu
from jax.sharding import PartitionSpec as P

SLOPE = 0.3
GROUP = 4
CHUNKS = 2
TAPS = 128
MESH = pl.DeviceIdType.MESH


def tap_table(channels):
    table = np.zeros((TAPS, 8, 4, 4, 4, channels), np.float32)
    for cell in range(8):
        a, b, g = cell // 4, (cell // 2) % 2, cell % 2
        for tap in range(channels * 27):
            c, i, j, k = tap // 27, (tap // 9) % 3, (tap // 3) % 3, tap % 3
            table[tap, cell, g + k, b + j, a + i, c] = 1.0
    return table.reshape(TAPS, 8 * 64 * channels)


def dot(left, right, dims=((1,), (0,)), precision=None):
    return lax.dot_general(left, right, (dims, ((), ())), precision=precision, preferred_element_type=jnp.float32)


def greet(barrier, space, groups, s, f):
    for d in range(1, space):
        pl.semaphore_signal(barrier, inc=1, device_id=(lax.rem(s + d, space), f), device_id_type=MESH)
    for e in range(1, groups):
        pl.semaphore_signal(barrier, inc=1, device_id=(s, lax.rem(f + e, groups)), device_id_type=MESH)


def push(source, target, sems, index, device):
    send, recv = sems
    return pltpu.make_async_remote_copy(
        src_ref=source, dst_ref=target, send_sem=send.at[index], recv_sem=recv.at[index], device_id=device, device_id_type=MESH
    )


def when_sent(there, here, copy):
    @pl.when(there)
    def _():
        copy.wait_send()

    @pl.when(here)
    def _():
        copy.wait_recv()


def halo(s, count, ahead, back, filled, emptied):
    @pl.when(s < count - 1)
    def _():
        ahead.start()

    @pl.when(s > 0)
    def _():
        back.start()

    @pl.when(s == 0)
    def _():
        filled[...] = jnp.zeros_like(filled)

    @pl.when(s == count - 1)
    def _():
        emptied[...] = jnp.zeros_like(emptied)


def section(
    space, groups, vol, up, taps, table, second, moved, sums,
    before, after, above, below, tail, head, up_mid, up_here, pooled, pool_mid,
    cells, first_mat, back_mat, windows, actives, g_first, g_second, grads, g_mid, g_sum, g_all,
    h_send, h_recv, uz_send, uz_recv, uf_send, uf_recv, pf_send, pf_recv, pz_send, pz_recv, gf_send, gf_recv, gz_send, gz_recv,
):
    s, f = lax.axis_index("space"), lax.axis_index("filt")
    channels, planes, rows, cols = vol.shape
    parts = space // groups
    window = channels * 4
    half = cols // 2
    lanes = half // 128
    filters, outputs = taps.shape[0], second.shape[0]
    own = filters // groups
    group_out, band = up.shape[1:]
    size = 16 * window
    width = GROUP * half
    per_part = band // width
    per_chunk = per_part // CHUNKS
    barrier = pltpu.get_barrier_semaphore()
    greet(barrier, space, groups, s, f)
    for cell in range(8):
        first_mat[cell * filters:(cell + 1) * filters, :] = dot(taps[...], table[:, cell * size:(cell + 1) * size]).astype(jnp.bfloat16)
    back_mat[...] = second[...].astype(jnp.float32).T.astype(jnp.bfloat16)
    g_first[...] = jnp.zeros_like(g_first)
    g_second[...] = jnp.zeros_like(g_second)
    pl.semaphore_wait(barrier, space + groups - 2)

    sems = (h_send, h_recv)
    ahead = push(vol.at[:, planes - 1], before, sems, 0, (jnp.minimum(s + 1, space - 1), f))
    back = push(vol.at[:, 0], after, sems, 1, (jnp.maximum(s - 1, 0), f))
    halo(s, space, ahead, back, before, after)
    up_moves = [[] for _ in range(CHUNKS)]
    for k in range(CHUNKS):
        chunk = pl.ds(k * per_chunk * width, per_chunk * width)
        for d in range(1, space):
            peer = lax.rem(s + d, space)
            up_moves[k].append(push(up.at[peer, :, chunk], up_mid.at[s, :, chunk], (uz_send, uz_recv), k * space + d, (peer, f)))
            up_moves[k][-1].start()
    up_mid[s] = up[s]

    source = lax.broadcasted_iota(jnp.int32, (cols, 4 * half), 0)
    target = lax.broadcasted_iota(jnp.int32, (cols, 4 * half), 1)
    pick = (source == 2 * lax.rem(target, half) + lax.div(target, half) - 1).astype(jnp.float32).astype(jnp.bfloat16)

    def fill(dz):
        for c in range(channels):
            plane = before[c] if dz == 0 else after[c] if dz == 3 else vol[c, dz - 1]
            spread = dot(plane, pick)
            for lane in range(4 * lanes):
                cells[lane, pl.ds(window + dz * channels + c, rows, stride=window), :] = spread[:, lane * 128:(lane + 1) * 128]

    fill(1)
    when_sent(s < space - 1, s > 0, ahead)
    when_sent(s > 0, s < space - 1, back)

    def edge(row):
        lines = [
            (before[c] if dz == 0 else after[c] if dz == 3 else vol[c, dz - 1])[row:row + 1, :].astype(jnp.float32)
            for dz in range(4)
            for c in range(channels)
        ]
        return jnp.concatenate(lines, axis=0).astype(jnp.bfloat16)

    tail[...] = edge(rows - 1)
    head[...] = edge(0)
    down = push(tail, above, sems, 2, (s, jnp.minimum(f + 1, groups - 1)))
    upward = push(head, below, sems, 3, (s, jnp.maximum(f - 1, 0)))
    halo(f, groups, down, upward, above, below)
    fill(0)
    fill(2)
    fill(3)
    when_sent(f < groups - 1, f > 0, down)
    when_sent(f > 0, f < groups - 1, upward)
    for border, at in ((above, 0), (below, window * (rows + 1))):
        spread = dot(border[...], pick)
        for lane in range(4 * lanes):
            cells[lane, at:at + window, :] = spread[:, lane * 128:(lane + 1) * 128]

    pool_turns = []
    for part in range(parts):

        def forward(index, carry):
            place = part * per_part + index
            columns = []
            for y in range(GROUP):
                start = pl.multiple_of((place * GROUP + y) * 2 * window, 2 * window)
                tiles = [
                    jnp.concatenate(
                        [cells[dx * lanes + lane, pl.ds(start, 4 * window), :].astype(jnp.bfloat16) for lane in range(lanes)], axis=1
                    )
                    for dx in range(4)
                ]
                columns.append(jnp.concatenate(tiles, axis=0))
            patches = jnp.concatenate(columns, axis=1)
            windows[place] = patches
            first_out = dot(first_mat[...], patches)
            active = jnp.where(first_out > 0, first_out, SLOPE * first_out).astype(jnp.bfloat16)
            actives[place] = active
            pooled_tile = dot(second[...], active).astype(jnp.bfloat16)
            span = pl.ds(pl.multiple_of(index * width, width), width)
            for group in range(groups):
                pooled[group, part, :, span] = pooled_tile[group * group_out:(group + 1) * group_out]
            return carry

        lax.fori_loop(0, per_part, forward, 0)
        for e in range(1, groups):
            peer = lax.rem(f + e, groups)
            pool_turns.append(push(pooled.at[peer, part], pool_mid.at[f * parts + part], (pf_send, pf_recv), part * groups + e, (s, peer)))
            pool_turns[-1].start()
        pool_mid[f * parts + part] = pooled[f, part]

    def backward(index, k):
        part = index // per_chunk
        inner = k * per_chunk + index % per_chunk
        place = part * per_part + inner
        span = pl.ds(pl.multiple_of(inner * width, width), width)
        active = actives[place]
        gradient = jnp.concatenate([up_here[group, part, :, span] for group in range(groups)], axis=0)
        back_flow = dot(back_mat[...], gradient)
        steered = (back_flow * jnp.where(active.astype(jnp.float32) > 0, 1.0, SLOPE)).astype(jnp.bfloat16)
        g_second[...] += dot(active, gradient, ((1,), (1,)))
        g_first[...] += dot(steered, windows[place], ((1,), (1,)))
        return k

    pool_moves = []
    for k in range(CHUNKS):
        chunk = pl.ds(k * per_chunk * width, per_chunk * width)
        for move in up_moves[k]:
            move.wait()
        up_turns = []
        for e in range(1, groups):
            peer = lax.rem(f + e, groups)
            up_turns.append(
                push(up_mid.at[pl.ds(peer * parts, parts), :, chunk], up_here.at[f, :, :, chunk], (uf_send, uf_recv), k * groups + e, (s, peer))
            )
            up_turns[-1].start()
        up_here[f, :, :, chunk] = up_mid[pl.ds(f * parts, parts), :, chunk]
        if k == CHUNKS - 1:
            for turn in pool_turns:
                turn.wait()
            for d in range(1, space):
                peer = lax.rem(s + d, space)
                pool_moves.append(push(pool_mid.at[peer], moved.at[s], (pz_send, pz_recv), d, (peer, f)))
                pool_moves[-1].start()
            moved[s] = pool_mid[s]
        for turn in up_turns:
            turn.wait()
        lax.fori_loop(0, parts * per_chunk, lambda index, carry, k=k: (backward(index, k), carry)[1], 0)

    grads[...] = jnp.zeros_like(grads)
    total = jnp.zeros((filters, TAPS), jnp.float32)
    for cell in range(8):
        piece = table[:, cell * size:(cell + 1) * size].astype(jnp.float32)
        total += dot(g_first[cell * filters:(cell + 1) * filters, :], piece, ((1,), (1,)), lax.Precision.HIGHEST)
    for group in range(groups):
        for cell in range(8):
            first = cell * filters + group * own
            grads[group, cell, :, 0:outputs] = g_second[first:first + own, :]
        grads[group, 8, :, :] = total[group * own:(group + 1) * own]
    g_turns = []
    for e in range(1, groups):
        peer = lax.rem(f + e, groups)
        g_turns.append(push(grads.at[peer], g_mid.at[f], (gf_send, gf_recv), e, (s, peer)))
        g_turns[-1].start()
    g_mid[f] = grads[f]
    for turn in g_turns:
        turn.wait()
    total = g_mid[0]
    for group in range(1, groups):
        total = total + g_mid[group]
    g_sum[...] = total
    g_moves = []
    for d in range(1, space):
        peer = lax.rem(s + d, space)
        g_moves.append(push(g_sum, g_all.at[s], (gz_send, gz_recv), d, (peer, f)))
        g_moves[-1].start()
    g_all[s] = total
    for move in g_moves:
        move.wait()
    total = g_all[0]
    for place in range(1, space):
        total = total + g_all[place]
    sums[...] = total
    for move in pool_moves:
        move.wait()


def shards(volume, first_kernel, second_kernel, upstream):
    space, groups = lax.axis_size("space"), lax.axis_size("filt")
    channels, planes, rows, cols = volume.shape
    filters, outputs = first_kernel.shape[0], second_kernel.shape[0]
    group_out, depth_out, band = upstream.shape
    parts = space // groups
    own = filters // groups
    half = cols // 2
    window = 4 * channels
    vmem = pl.BlockSpec(memory_space=pltpu.VMEM)
    half_type = lambda *shape: jax.ShapeDtypeStruct(shape, jnp.bfloat16)
    dma = lambda *counts: [pltpu.SemaphoreType.DMA((count,)) for count in counts for _ in range(2)]

    taps = jnp.pad(first_kernel.reshape(filters, channels * 27), ((0, 0), (0, TAPS - channels * 27)))
    table = jnp.asarray(tap_table(channels), jnp.bfloat16)
    second = second_kernel.transpose(0, 2, 3, 4, 1).reshape(outputs, 8 * filters)
    depth = 8 * filters
    steps = rows // 2 // GROUP
    bf16 = lambda *shape: pltpu.VMEM(shape, jnp.bfloat16)
    f32 = lambda *shape: pltpu.VMEM(shape, jnp.float32)
    moved, sums = pl.pallas_call(
        functools.partial(section, space, groups),
        out_shape=(half_type(space, group_out, band), jax.ShapeDtypeStruct((9, own, TAPS), jnp.float32)),
        in_specs=[vmem] * 5,
        out_specs=(vmem, vmem),
        scratch_shapes=[
            bf16(channels, rows, cols),
            bf16(channels, rows, cols),
            *[bf16(window, cols) for _ in range(4)],
            bf16(space, group_out, band),
            bf16(groups, parts, group_out, band),
            bf16(groups, parts, group_out, band),
            bf16(space, group_out, band),
            f32(4 * half // 128, window * (rows + 2), 128),
            bf16(depth, 16 * window),
            bf16(depth, outputs),
            bf16(steps, 16 * window, GROUP * half),
            bf16(steps, depth, GROUP * half),
            f32(depth, 16 * window),
            f32(depth, outputs),
            f32(groups, 9, own, TAPS),
            f32(groups, 9, own, TAPS),
            f32(9, own, TAPS),
            f32(space, 9, own, TAPS),
            *dma(4, CHUNKS * space, CHUNKS * groups, parts * groups, space, groups, space),
        ],
        compiler_params=pltpu.CompilerParams(collective_id=0, has_side_effects=True, vmem_limit_bytes=56 * 2**20),
        cost_estimate=pl.CostEstimate(flops=6 * 10**9, bytes_accessed=4 * 10**6, transcendentals=0),
        name="section",
    )(volume, upstream.transpose(1, 0, 2), taps, table, second)
    grad_first = sums[8, :, 0:channels * 27].reshape(own, channels, 3, 3, 3)
    grad_second = sums[0:8, :, 0:outputs].transpose(2, 1, 0).reshape(outputs, own, 2, 2, 2)
    return (moved.transpose(1, 0, 2), grad_first, grad_second)


def solution(mesh):
    in_specs = (P(None, "space", "filt", None), P(), P(), P("filt", None, "space"))
    out_specs = (
        P("filt", None, "space"),
        P("filt", None, None, None, None),
        P(None, "filt", None, None, None),
    )
    return jax.shard_map(shards, mesh=mesh, in_specs=in_specs, out_specs=out_specs, check_vma=False)
```

```python
import functools

import jax
import jax.numpy as jnp
import numpy as np
from jax import lax
from jax.experimental import pallas as pl
from jax.experimental.pallas import tpu as pltpu
from jax.sharding import PartitionSpec as P

SLOPE = 0.3
GROUP = 4
CHUNKS = 2
TAPS = 128
MESH = pl.DeviceIdType.MESH


def tap_table(channels):
    table = np.zeros((TAPS, 8, 4, 4, 4, channels), np.float32)
    for cell in range(8):
        a, b, g = cell // 4, (cell // 2) % 2, cell % 2
        for tap in range(channels * 27):
            c, i, j, k = tap // 27, (tap // 9) % 3, (tap // 3) % 3, tap % 3
            table[tap, cell, g + k, b + j, a + i, c] = 1.0
    return table.reshape(TAPS, 8 * 64 * channels)


def dot(left, right, dims=((1,), (0,)), precision=None):
    return lax.dot_general(left, right, (dims, ((), ())), precision=precision, preferred_element_type=jnp.float32)


def greet(barrier, space, groups, s, f):
    for d in range(1, space):
        pl.semaphore_signal(barrier, inc=1, device_id=(lax.rem(s + d, space), f), device_id_type=MESH)
    for e in range(1, groups):
        pl.semaphore_signal(barrier, inc=1, device_id=(s, lax.rem(f + e, groups)), device_id_type=MESH)


def push(source, target, sems, index, device):
    send, recv = sems
    return pltpu.make_async_remote_copy(
        src_ref=source, dst_ref=target, send_sem=send.at[index], recv_sem=recv.at[index], device_id=device, device_id_type=MESH
    )


def when_sent(there, here, copy):
    @pl.when(there)
    def _():
        copy.wait_send()

    @pl.when(here)
    def _():
        copy.wait_recv()


def halo(s, count, ahead, back, filled, emptied):
    @pl.when(s < count - 1)
    def _():
        ahead.start()

    @pl.when(s > 0)
    def _():
        back.start()

    @pl.when(s == 0)
    def _():
        filled[...] = jnp.zeros_like(filled)

    @pl.when(s == count - 1)
    def _():
        emptied[...] = jnp.zeros_like(emptied)


def section(
    space, groups, vol, up, taps, table, second, moved, sums,
    before, after, above, below, tail, head, up_mid, up_here, pooled, pool_mid,
    cells, first_mat, back_mat, windows, actives, g_first, g_second, grads, g_mid, g_sum, g_all,
    h_send, h_recv, uz_send, uz_recv, uf_send, uf_recv, pf_send, pf_recv, pz_send, pz_recv, gf_send, gf_recv, gz_send, gz_recv,
):
    s, f = lax.axis_index("space"), lax.axis_index("filt")
    channels, planes, rows, cols = vol.shape
    parts = space // groups
    window = channels * 4
    half = cols // 2
    lanes = half // 128
    filters, outputs = taps.shape[0], second.shape[0]
    own = filters // groups
    group_out, band = up.shape[1:]
    size = 16 * window
    width = GROUP * half
    per_part = band // width
    per_chunk = per_part // CHUNKS
    barrier = pltpu.get_barrier_semaphore()
    greet(barrier, space, groups, s, f)
    for cell in range(8):
        first_mat[cell * filters:(cell + 1) * filters, :] = dot(taps[...], table[:, cell * size:(cell + 1) * size]).astype(jnp.bfloat16)
    back_mat[...] = second[...].astype(jnp.float32).T.astype(jnp.bfloat16)
    g_first[...] = jnp.zeros_like(g_first)
    g_second[...] = jnp.zeros_like(g_second)
    pl.semaphore_wait(barrier, space + groups - 2)

    sems = (h_send, h_recv)
    ahead = push(vol.at[:, planes - 1], before, sems, 0, (jnp.minimum(s + 1, space - 1), f))
    back = push(vol.at[:, 0], after, sems, 1, (jnp.maximum(s - 1, 0), f))
    halo(s, space, ahead, back, before, after)
    far_first = sorted(range(1, space), key=lambda d: (abs(2 * d - space), d))
    up_moves = [[] for _ in range(CHUNKS)]
    for k in range(CHUNKS):
        chunk = pl.ds(k * per_chunk * width, per_chunk * width)
        for d in far_first:
            peer = lax.rem(s + d, space)
            up_moves[k].append(push(up.at[peer, :, chunk], up_mid.at[s, :, chunk], (uz_send, uz_recv), k * space + d, (peer, f)))
            up_moves[k][-1].start()
    up_mid[s] = up[s]

    source = lax.broadcasted_iota(jnp.int32, (cols, 4 * half), 0)
    target = lax.broadcasted_iota(jnp.int32, (cols, 4 * half), 1)
    pick = (source == 2 * lax.rem(target, half) + lax.div(target, half) - 1).astype(jnp.float32).astype(jnp.bfloat16)

    def fill(dz):
        for c in range(channels):
            plane = before[c] if dz == 0 else after[c] if dz == 3 else vol[c, dz - 1]
            spread = dot(plane, pick)
            for lane in range(4 * lanes):
                cells[lane, pl.ds(window + dz * channels + c, rows, stride=window), :] = spread[:, lane * 128:(lane + 1) * 128]

    fill(1)
    when_sent(s < space - 1, s > 0, ahead)
    when_sent(s > 0, s < space - 1, back)

    def edge(row):
        lines = [
            (before[c] if dz == 0 else after[c] if dz == 3 else vol[c, dz - 1])[row:row + 1, :].astype(jnp.float32)
            for dz in range(4)
            for c in range(channels)
        ]
        return jnp.concatenate(lines, axis=0).astype(jnp.bfloat16)

    tail[...] = edge(rows - 1)
    head[...] = edge(0)
    down = push(tail, above, sems, 2, (s, jnp.minimum(f + 1, groups - 1)))
    upward = push(head, below, sems, 3, (s, jnp.maximum(f - 1, 0)))
    halo(f, groups, down, upward, above, below)
    fill(0)
    fill(2)
    fill(3)
    when_sent(f < groups - 1, f > 0, down)
    when_sent(f > 0, f < groups - 1, upward)
    for border, at in ((above, 0), (below, window * (rows + 1))):
        spread = dot(border[...], pick)
        for lane in range(4 * lanes):
            cells[lane, at:at + window, :] = spread[:, lane * 128:(lane + 1) * 128]

    pool_turns = []
    for part in range(parts):

        def forward(index, carry):
            place = part * per_part + index
            columns = []
            for y in range(GROUP):
                start = pl.multiple_of((place * GROUP + y) * 2 * window, 2 * window)
                tiles = [
                    jnp.concatenate(
                        [cells[dx * lanes + lane, pl.ds(start, 4 * window), :].astype(jnp.bfloat16) for lane in range(lanes)], axis=1
                    )
                    for dx in range(4)
                ]
                columns.append(jnp.concatenate(tiles, axis=0))
            patches = jnp.concatenate(columns, axis=1)
            windows[place] = patches
            first_out = dot(first_mat[...], patches)
            active = jnp.where(first_out > 0, first_out, SLOPE * first_out).astype(jnp.bfloat16)
            actives[place] = active
            pooled_tile = dot(second[...], active).astype(jnp.bfloat16)
            span = pl.ds(pl.multiple_of(index * width, width), width)
            for group in range(groups):
                pooled[group, part, :, span] = pooled_tile[group * group_out:(group + 1) * group_out]
            return carry

        lax.fori_loop(0, per_part, forward, 0)
        for e in range(1, groups):
            peer = lax.rem(f + e, groups)
            pool_turns.append(push(pooled.at[peer, part], pool_mid.at[f * parts + part], (pf_send, pf_recv), part * groups + e, (s, peer)))
            pool_turns[-1].start()
        pool_mid[f * parts + part] = pooled[f, part]

    def backward(index, k):
        part = index // per_chunk
        inner = k * per_chunk + index % per_chunk
        place = part * per_part + inner
        span = pl.ds(pl.multiple_of(inner * width, width), width)
        active = actives[place]
        gradient = jnp.concatenate([up_here[group, part, :, span] for group in range(groups)], axis=0)
        back_flow = dot(back_mat[...], gradient)
        steered = (back_flow * jnp.where(active.astype(jnp.float32) > 0, 1.0, SLOPE)).astype(jnp.bfloat16)
        g_second[...] += dot(active, gradient, ((1,), (1,)))
        g_first[...] += dot(steered, windows[place], ((1,), (1,)))
        return k

    pool_moves = []

    def pool_start(until):
        for d in far_first[len(pool_moves):until]:
            peer = lax.rem(s + d, space)
            pool_moves.append(push(pool_mid.at[peer], moved.at[s], (pz_send, pz_recv), d, (peer, f)))
            pool_moves[-1].start()

    for k in range(CHUNKS):
        chunk = pl.ds(k * per_chunk * width, per_chunk * width)
        for move in up_moves[k]:
            move.wait()
        up_turns = []
        for e in range(1, groups):
            peer = lax.rem(f + e, groups)
            up_turns.append(
                push(up_mid.at[pl.ds(peer * parts, parts), :, chunk], up_here.at[f, :, :, chunk], (uf_send, uf_recv), k * groups + e, (s, peer))
            )
            up_turns[-1].start()
        up_here[f, :, :, chunk] = up_mid[pl.ds(f * parts, parts), :, chunk]
        if k == 0:
            for turn in pool_turns:
                turn.wait()
        pool_start((k + 1) * space // (2 * CHUNKS))
        for turn in up_turns:
            turn.wait()
        lax.fori_loop(0, parts * per_chunk, lambda index, carry, k=k: (backward(index, k), carry)[1], 0)

    grads[...] = jnp.zeros_like(grads)
    total = jnp.zeros((filters, TAPS), jnp.float32)
    for cell in range(8):
        piece = table[:, cell * size:(cell + 1) * size].astype(jnp.float32)
        total += dot(g_first[cell * filters:(cell + 1) * filters, :], piece, ((1,), (1,)), lax.Precision.HIGHEST)
    for group in range(groups):
        for cell in range(8):
            first = cell * filters + group * own
            grads[group, cell, :, 0:outputs] = g_second[first:first + own, :]
        grads[group, 8, :, :] = total[group * own:(group + 1) * own]
    g_turns = []
    for e in range(1, groups):
        peer = lax.rem(f + e, groups)
        g_turns.append(push(grads.at[peer], g_mid.at[f], (gf_send, gf_recv), e, (s, peer)))
        g_turns[-1].start()
    pool_start(5 * space // 8)
    g_mid[f] = grads[f]
    for turn in g_turns:
        turn.wait()
    total = g_mid[0]
    for group in range(1, groups):
        total = total + g_mid[group]
    g_sum[...] = total
    g_moves = []
    for d in range(1, space):
        peer = lax.rem(s + d, space)
        g_moves.append(push(g_sum, g_all.at[s], (gz_send, gz_recv), d, (peer, f)))
        g_moves[-1].start()
    pool_start(space)
    moved[s] = pool_mid[s]
    g_all[s] = total
    for move in g_moves:
        move.wait()
    total = g_all[0]
    for place in range(1, space):
        total = total + g_all[place]
    sums[...] = total
    for move in pool_moves:
        move.wait()


def shards(volume, first_kernel, second_kernel, upstream):
    space, groups = lax.axis_size("space"), lax.axis_size("filt")
    channels, planes, rows, cols = volume.shape
    filters, outputs = first_kernel.shape[0], second_kernel.shape[0]
    group_out, depth_out, band = upstream.shape
    parts = space // groups
    own = filters // groups
    half = cols // 2
    window = 4 * channels
    vmem = pl.BlockSpec(memory_space=pltpu.VMEM)
    half_type = lambda *shape: jax.ShapeDtypeStruct(shape, jnp.bfloat16)
    dma = lambda *counts: [pltpu.SemaphoreType.DMA((count,)) for count in counts for _ in range(2)]

    taps = jnp.pad(first_kernel.reshape(filters, channels * 27), ((0, 0), (0, TAPS - channels * 27)))
    table = jnp.asarray(tap_table(channels), jnp.bfloat16)
    second = second_kernel.transpose(0, 2, 3, 4, 1).reshape(outputs, 8 * filters)
    depth = 8 * filters
    steps = rows // 2 // GROUP
    bf16 = lambda *shape: pltpu.VMEM(shape, jnp.bfloat16)
    f32 = lambda *shape: pltpu.VMEM(shape, jnp.float32)
    moved, sums = pl.pallas_call(
        functools.partial(section, space, groups),
        out_shape=(half_type(space, group_out, band), jax.ShapeDtypeStruct((9, own, TAPS), jnp.float32)),
        in_specs=[vmem] * 5,
        out_specs=(vmem, vmem),
        scratch_shapes=[
            bf16(channels, rows, cols),
            bf16(channels, rows, cols),
            *[bf16(window, cols) for _ in range(4)],
            bf16(space, group_out, band),
            bf16(groups, parts, group_out, band),
            bf16(groups, parts, group_out, band),
            bf16(space, group_out, band),
            f32(4 * half // 128, window * (rows + 2), 128),
            bf16(depth, 16 * window),
            bf16(depth, outputs),
            bf16(steps, 16 * window, GROUP * half),
            bf16(steps, depth, GROUP * half),
            f32(depth, 16 * window),
            f32(depth, outputs),
            f32(groups, 9, own, TAPS),
            f32(groups, 9, own, TAPS),
            f32(9, own, TAPS),
            f32(space, 9, own, TAPS),
            *dma(4, CHUNKS * space, CHUNKS * groups, parts * groups, space, groups, space),
        ],
        compiler_params=pltpu.CompilerParams(collective_id=0, has_side_effects=True, vmem_limit_bytes=56 * 2**20),
        cost_estimate=pl.CostEstimate(flops=6 * 10**9, bytes_accessed=4 * 10**6, transcendentals=0),
        name="section",
    )(volume, upstream.transpose(1, 0, 2), taps, table, second)
    grad_first = sums[8, :, 0:channels * 27].reshape(own, channels, 3, 3, 3)
    grad_second = sums[0:8, :, 0:outputs].transpose(2, 1, 0).reshape(outputs, own, 2, 2, 2)
    return (moved.transpose(1, 0, 2), grad_first, grad_second)


def solution(mesh):
    in_specs = (P(None, "space", "filt", None), P(), P(), P("filt", None, "space"))
    out_specs = (
        P("filt", None, "space"),
        P("filt", None, None, None, None),
        P(None, "filt", None, None, None),
    )
    return jax.shard_map(shards, mesh=mesh, in_specs=in_specs, out_specs=out_specs, check_vma=False)
```

```python
import functools

import jax
import jax.numpy as jnp
import numpy as np
from jax import lax
from jax.experimental import pallas as pl
from jax.experimental.pallas import tpu as pltpu
from jax.sharding import PartitionSpec as P

SLOPE = 0.3
GROUP = 4
CHUNKS = 2
TAPS = 128
MESH = pl.DeviceIdType.MESH


def tap_table(channels):
    table = np.zeros((TAPS, 8, 4, 4, 4, channels), np.float32)
    for cell in range(8):
        a, b, g = cell // 4, (cell // 2) % 2, cell % 2
        for tap in range(channels * 27):
            c, i, j, k = tap // 27, (tap // 9) % 3, (tap // 3) % 3, tap % 3
            table[tap, cell, g + k, b + j, a + i, c] = 1.0
    return table.reshape(TAPS, 8 * 64 * channels)


def dot(left, right, dims=((1,), (0,)), precision=None):
    return lax.dot_general(left, right, (dims, ((), ())), precision=precision, preferred_element_type=jnp.float32)


def greet(barrier, space, groups, s, f):
    for d in range(1, space):
        pl.semaphore_signal(barrier, inc=1, device_id=(lax.rem(s + d, space), f), device_id_type=MESH)
    for e in range(1, groups):
        pl.semaphore_signal(barrier, inc=1, device_id=(s, lax.rem(f + e, groups)), device_id_type=MESH)


def push(source, target, sems, index, device):
    send, recv = sems
    return pltpu.make_async_remote_copy(
        src_ref=source, dst_ref=target, send_sem=send.at[index], recv_sem=recv.at[index], device_id=device, device_id_type=MESH
    )


def when_sent(there, here, copy):
    @pl.when(there)
    def _():
        copy.wait_send()

    @pl.when(here)
    def _():
        copy.wait_recv()


def halo(s, count, ahead, back, filled, emptied):
    @pl.when(s < count - 1)
    def _():
        ahead.start()

    @pl.when(s > 0)
    def _():
        back.start()

    @pl.when(s == 0)
    def _():
        filled[...] = jnp.zeros_like(filled)

    @pl.when(s == count - 1)
    def _():
        emptied[...] = jnp.zeros_like(emptied)


def section(
    space, groups, vol, up, taps, table, second, moved, sums,
    before, after, above, below, tail, head, up_mid, up_here, pooled, pool_mid,
    cells, first_mat, back_mat, windows, actives, g_first, g_second, grads, g_mid, g_sum, g_all,
    h_send, h_recv, uz_send, uz_recv, uf_send, uf_recv, pf_send, pf_recv, pz_send, pz_recv, gf_send, gf_recv, gz_send, gz_recv,
):
    s, f = lax.axis_index("space"), lax.axis_index("filt")
    channels, planes, rows, cols = vol.shape
    parts = space // groups
    window = channels * 4
    half = cols // 2
    lanes = half // 128
    filters, outputs = taps.shape[0], second.shape[0]
    own = filters // groups
    group_out, band = up.shape[1:]
    size = 16 * window
    width = GROUP * half
    per_part = band // width
    per_chunk = per_part // CHUNKS
    barrier = pltpu.get_barrier_semaphore()
    greet(barrier, space, groups, s, f)
    for cell in range(8):
        first_mat[cell * filters:(cell + 1) * filters, :] = dot(taps[...], table[:, cell * size:(cell + 1) * size]).astype(jnp.bfloat16)
    back_mat[...] = second[...].astype(jnp.float32).T.astype(jnp.bfloat16)
    g_first[...] = jnp.zeros_like(g_first)
    g_second[...] = jnp.zeros_like(g_second)
    pl.semaphore_wait(barrier, space + groups - 2)

    sems = (h_send, h_recv)
    ahead = push(vol.at[:, planes - 1], before, sems, 0, (jnp.minimum(s + 1, space - 1), f))
    back = push(vol.at[:, 0], after, sems, 1, (jnp.maximum(s - 1, 0), f))
    halo(s, space, ahead, back, before, after)
    far_first = sorted(range(1, space), key=lambda d: (abs(2 * d - space), d))
    up_moves = [[] for _ in range(CHUNKS)]
    for k in range(CHUNKS):
        chunk = pl.ds(k * per_chunk * width, per_chunk * width)
        for d in far_first:
            peer = lax.rem(s + d, space)
            up_moves[k].append(push(up.at[peer, :, chunk], up_mid.at[s, :, chunk], (uz_send, uz_recv), k * space + d, (peer, f)))
            up_moves[k][-1].start()
    up_mid[s] = up[s]

    source = lax.broadcasted_iota(jnp.int32, (cols, 4 * half), 0)
    target = lax.broadcasted_iota(jnp.int32, (cols, 4 * half), 1)
    pick = (source == 2 * lax.rem(target, half) + lax.div(target, half) - 1).astype(jnp.float32).astype(jnp.bfloat16)

    def fill(dz):
        for c in range(channels):
            plane = before[c] if dz == 0 else after[c] if dz == 3 else vol[c, dz - 1]
            spread = dot(plane, pick)
            for lane in range(4 * lanes):
                cells[lane, pl.ds(window + dz * channels + c, rows, stride=window), :] = spread[:, lane * 128:(lane + 1) * 128]

    fill(1)
    when_sent(s < space - 1, s > 0, ahead)
    when_sent(s > 0, s < space - 1, back)

    def edge(row):
        lines = [
            (before[c] if dz == 0 else after[c] if dz == 3 else vol[c, dz - 1])[row:row + 1, :].astype(jnp.float32)
            for dz in range(4)
            for c in range(channels)
        ]
        return jnp.concatenate(lines, axis=0).astype(jnp.bfloat16)

    tail[...] = edge(rows - 1)
    head[...] = edge(0)
    down = push(tail, above, sems, 2, (s, jnp.minimum(f + 1, groups - 1)))
    upward = push(head, below, sems, 3, (s, jnp.maximum(f - 1, 0)))
    halo(f, groups, down, upward, above, below)
    fill(0)
    fill(2)
    fill(3)
    when_sent(f < groups - 1, f > 0, down)
    when_sent(f > 0, f < groups - 1, upward)
    for border, at in ((above, 0), (below, window * (rows + 1))):
        spread = dot(border[...], pick)
        for lane in range(4 * lanes):
            cells[lane, at:at + window, :] = spread[:, lane * 128:(lane + 1) * 128]

    pool_turns = []
    for part in range(parts):

        def forward(index, carry):
            place = part * per_part + index
            columns = []
            for y in range(GROUP):
                start = pl.multiple_of((place * GROUP + y) * 2 * window, 2 * window)
                tiles = [
                    jnp.concatenate(
                        [cells[dx * lanes + lane, pl.ds(start, 4 * window), :].astype(jnp.bfloat16) for lane in range(lanes)], axis=1
                    )
                    for dx in range(4)
                ]
                columns.append(jnp.concatenate(tiles, axis=0))
            patches = jnp.concatenate(columns, axis=1)
            windows[place] = patches
            first_out = dot(first_mat[...], patches)
            active = jnp.where(first_out > 0, first_out, SLOPE * first_out).astype(jnp.bfloat16)
            actives[place] = active
            pooled_tile = dot(second[...], active).astype(jnp.bfloat16)
            span = pl.ds(pl.multiple_of(index * width, width), width)
            for group in range(groups):
                pooled[group, part, :, span] = pooled_tile[group * group_out:(group + 1) * group_out]
            return carry

        lax.fori_loop(0, per_part, forward, 0)
        for e in range(1, groups):
            peer = lax.rem(f + e, groups)
            pool_turns.append(push(pooled.at[peer, part], pool_mid.at[f * parts + part], (pf_send, pf_recv), part * groups + e, (s, peer)))
            pool_turns[-1].start()
        pool_mid[f * parts + part] = pooled[f, part]

    def backward(index, k):
        part = index // per_chunk
        inner = k * per_chunk + index % per_chunk
        place = part * per_part + inner
        span = pl.ds(pl.multiple_of(inner * width, width), width)
        active = actives[place]
        gradient = jnp.concatenate([up_here[group, part, :, span] for group in range(groups)], axis=0)
        back_flow = dot(back_mat[...], gradient)
        steered = (back_flow * jnp.where(active.astype(jnp.float32) > 0, 1.0, SLOPE)).astype(jnp.bfloat16)
        g_second[...] += dot(active, gradient, ((1,), (1,)))
        g_first[...] += dot(steered, windows[place], ((1,), (1,)))
        return k

    pool_moves = []

    def pool_start(until):
        for d in far_first[len(pool_moves):until]:
            peer = lax.rem(s + d, space)
            pool_moves.append(push(pool_mid.at[peer], moved.at[s], (pz_send, pz_recv), d, (peer, f)))
            pool_moves[-1].start()

    for k in range(CHUNKS):
        chunk = pl.ds(k * per_chunk * width, per_chunk * width)
        for move in up_moves[k]:
            move.wait()
        up_turns = []
        for e in range(1, groups):
            peer = lax.rem(f + e, groups)
            up_turns.append(
                push(up_mid.at[pl.ds(peer * parts, parts), :, chunk], up_here.at[f, :, :, chunk], (uf_send, uf_recv), k * groups + e, (s, peer))
            )
            up_turns[-1].start()
        up_here[f, :, :, chunk] = up_mid[pl.ds(f * parts, parts), :, chunk]
        if k == 0:
            for turn in pool_turns:
                turn.wait()
        pool_start(3 * (k + 1) * space // (4 * CHUNKS))
        for turn in up_turns:
            turn.wait()
        lax.fori_loop(0, parts * per_chunk, lambda index, carry, k=k: (backward(index, k), carry)[1], 0)

    grads[...] = jnp.zeros_like(grads)
    total = jnp.zeros((filters, TAPS), jnp.float32)
    for cell in range(8):
        piece = table[:, cell * size:(cell + 1) * size].astype(jnp.float32)
        total += dot(g_first[cell * filters:(cell + 1) * filters, :], piece, ((1,), (1,)), lax.Precision.HIGHEST)
    for group in range(groups):
        for cell in range(8):
            first = cell * filters + group * own
            grads[group, cell, :, 0:outputs] = g_second[first:first + own, :]
        grads[group, 8, :, :] = total[group * own:(group + 1) * own]
    g_turns = []
    for e in range(1, groups):
        peer = lax.rem(f + e, groups)
        g_turns.append(push(grads.at[peer], g_mid.at[f], (gf_send, gf_recv), e, (s, peer)))
        g_turns[-1].start()
    g_mid[f] = grads[f]
    for turn in g_turns:
        turn.wait()
    total = g_mid[0]
    for group in range(1, groups):
        total = total + g_mid[group]
    g_sum[...] = total
    g_moves = []
    for d in range(1, space):
        peer = lax.rem(s + d, space)
        g_moves.append(push(g_sum, g_all.at[s], (gz_send, gz_recv), d, (peer, f)))
        g_moves[-1].start()
    pool_start(space)
    moved[s] = pool_mid[s]
    g_all[s] = total
    for move in g_moves:
        move.wait()
    total = g_all[0]
    for place in range(1, space):
        total = total + g_all[place]
    sums[...] = total
    for move in pool_moves:
        move.wait()


def shards(volume, first_kernel, second_kernel, upstream):
    space, groups = lax.axis_size("space"), lax.axis_size("filt")
    channels, planes, rows, cols = volume.shape
    filters, outputs = first_kernel.shape[0], second_kernel.shape[0]
    group_out, depth_out, band = upstream.shape
    parts = space // groups
    own = filters // groups
    half = cols // 2
    window = 4 * channels
    vmem = pl.BlockSpec(memory_space=pltpu.VMEM)
    half_type = lambda *shape: jax.ShapeDtypeStruct(shape, jnp.bfloat16)
    dma = lambda *counts: [pltpu.SemaphoreType.DMA((count,)) for count in counts for _ in range(2)]

    taps = jnp.pad(first_kernel.reshape(filters, channels * 27), ((0, 0), (0, TAPS - channels * 27)))
    table = jnp.asarray(tap_table(channels), jnp.bfloat16)
    second = second_kernel.transpose(0, 2, 3, 4, 1).reshape(outputs, 8 * filters)
    depth = 8 * filters
    steps = rows // 2 // GROUP
    bf16 = lambda *shape: pltpu.VMEM(shape, jnp.bfloat16)
    f32 = lambda *shape: pltpu.VMEM(shape, jnp.float32)
    moved, sums = pl.pallas_call(
        functools.partial(section, space, groups),
        out_shape=(half_type(space, group_out, band), jax.ShapeDtypeStruct((9, own, TAPS), jnp.float32)),
        in_specs=[vmem] * 5,
        out_specs=(vmem, vmem),
        scratch_shapes=[
            bf16(channels, rows, cols),
            bf16(channels, rows, cols),
            *[bf16(window, cols) for _ in range(4)],
            bf16(space, group_out, band),
            bf16(groups, parts, group_out, band),
            bf16(groups, parts, group_out, band),
            bf16(space, group_out, band),
            f32(4 * half // 128, window * (rows + 2), 128),
            bf16(depth, 16 * window),
            bf16(depth, outputs),
            bf16(steps, 16 * window, GROUP * half),
            bf16(steps, depth, GROUP * half),
            f32(depth, 16 * window),
            f32(depth, outputs),
            f32(groups, 9, own, TAPS),
            f32(groups, 9, own, TAPS),
            f32(9, own, TAPS),
            f32(space, 9, own, TAPS),
            *dma(4, CHUNKS * space, CHUNKS * groups, parts * groups, space, groups, space),
        ],
        compiler_params=pltpu.CompilerParams(collective_id=0, has_side_effects=True, vmem_limit_bytes=56 * 2**20),
        cost_estimate=pl.CostEstimate(flops=6 * 10**9, bytes_accessed=4 * 10**6, transcendentals=0),
        name="section",
    )(volume, upstream.transpose(1, 0, 2), taps, table, second)
    grad_first = sums[8, :, 0:channels * 27].reshape(own, channels, 3, 3, 3)
    grad_second = sums[0:8, :, 0:outputs].transpose(2, 1, 0).reshape(outputs, own, 2, 2, 2)
    return (moved.transpose(1, 0, 2), grad_first, grad_second)


def solution(mesh):
    in_specs = (P(None, "space", "filt", None), P(), P(), P("filt", None, "space"))
    out_specs = (
        P("filt", None, "space"),
        P("filt", None, None, None, None),
        P(None, "filt", None, None, None),
    )
    return jax.shard_map(shards, mesh=mesh, in_specs=in_specs, out_specs=out_specs, check_vma=False)
```
